128 devices in a mesh: tm: 8 (over x_lo, y), feat: 16 (over z, x_hi, core).
Axes of the slice: x: 4 (x_hi: 2, x_lo: 2; x = x_hi * 2 + x_lo), y: 4, z: 4, core: 2. Of those that a mesh axis runs over, the one named last changes fastest.
Arguments:
- dictionary: bfloat16 [16384, 16384], P('tm', 'feat'), may hold values from -6 to 6
- eigvecs: bfloat16 [16384, 256], P('feat'), may hold values from -0.046875 to 0.046875
- snapshots: float32 [32768, 16384], P('feat', 'tm'), may hold values from -0.046875 to 0.046875
Outputs:
- modes: float32 [32768, 256], P(('feat', 'tm'))
The draws below stay inside these ranges and needn't reach their ends.
All inputs are finite; a program needn't handle non-finite values.
Results may differ from the reference program's by a relative error of at most 0.0003.
Values sent between devices are 32-bit elements; how exact they have to be, the bound alone decides.
A program may use at most 64 MiB of HBM per device.

```python
import jax
import jax.numpy as jnp
from jax import lax

FUNCS = 16384
MODES = 256
SNAPS = 16384
CELLS = 32768


def level_of(rng, shape, pieces, least, top_value):
    gain = 1.0
    for axis_at, blocks in pieces:
        heights = jax.random.uniform(jax.random.fold_in(jax.random.fold_in(rng, 6), axis_at), (blocks,), jnp.float32, least / len(pieces), top_value / len(pieces))
        gain = gain * jnp.repeat(jnp.exp(heights), shape[axis_at] // blocks).reshape((-1,) + (1,) * (len(shape) - 1 - axis_at))
    return gain


def centred(stream_key, dims, width, limit, pieces=(), held_as=jnp.bfloat16):
    values = width * jax.random.normal(stream_key, dims, jnp.float32)
    if pieces:
        values = values * level_of(stream_key, dims, pieces, -0.22, 0.18)
    return jnp.clip(values, -limit, limit).astype(held_as)


def setup_inputs(seed: int = 0) -> dict:
    keys = jax.random.split(jax.random.key(seed), 4)
    dictionary = centred(keys[0], (SNAPS, FUNCS), 1.0, 6.0, ((0, 8), (1, 16)))
    eigvecs = centred(keys[1], (FUNCS, MODES), FUNCS ** -0.5, 0.046875, ((0, 16),))
    snapshots = centred(keys[2], (CELLS, SNAPS), SNAPS ** -0.5, 0.046875, ((0, 16), (1, 8)), jnp.float32)
    return dict(dictionary=dictionary, eigvecs=eigvecs, snapshots=snapshots)


def reference(dictionary, eigvecs, snapshots):
    coefficients = jnp.dot(dictionary, eigvecs, preferred_element_type=jnp.float32)
    return jnp.dot(snapshots, coefficients, precision=lax.Precision.HIGHEST, preferred_element_type=jnp.float32)
```

```python
import jax
import jax.numpy as jnp
from jax import lax
from jax.experimental import pallas as pl
from jax.experimental.pallas import tpu as pltpu
from jax.sharding import PartitionSpec as P

MESH = pl.DeviceIdType.MESH
F32, BF16 = jnp.float32, jnp.bfloat16
HALF = 128
BLK = 256
COPIES = 160


def at(start, size, align=None):
    return pl.ds(start if align is None else pl.multiple_of(start, align), size)


def kernel(
    d_hbm, v_hbm, s_hbm, o_ref,
    d, v, sf, s_hi, s_lo, p_sib, q, r_core, r_az, r_bx, r_ax, r_bz, cf, w, m,
    r_ya, r_xb, r_xa, r_yb, ld, ss, rs,
):
    tm, ft = lax.axis_index("tm"), lax.axis_index("feat")
    xl, y = tm // 4, tm % 4
    z, xh, c = ft // 4, (ft // 2) % 2, ft % 2

    def to_z(k):
        return {"tm": tm, "feat": ((z + k) % 4) * 4 + xh * 2 + c}

    def to_y(k):
        return {"tm": xl * 4 + (y + k) % 4, "feat": ft}

    to_xh = {"tm": tm, "feat": z * 4 + (1 - xh) * 2 + c}
    to_xl = {"tm": (1 - xl) * 4 + y, "feat": ft}
    to_core = {"tm": tm, "feat": z * 4 + xh * 2 + (1 - c)}

    used = [0]
    sent = []

    def numbers(count):
        first = used[0]
        used[0] += count
        return first

    def copy_of(src, dst, sem, device):
        return pltpu.make_async_remote_copy(
            src_ref=src, dst_ref=dst, send_sem=ss.at[sem], recv_sem=rs.at[sem],
            device_id=device, device_id_type=MESH,
        )

    def send(src, dst, device):
        copy = copy_of(src, dst, numbers(1), device)
        copy.start()
        sent.append(copy)
        return copy

    load_v = pltpu.make_async_copy(v_hbm, v, ld.at[0])
    load_v.start()

    def load_d(i):
        rows = at(((1 - c) * 4 + i) % 8 * BLK, BLK, BLK)
        return pltpu.make_async_copy(d_hbm.at[rows], d.at[rows], ld.at[1 + i])

    def load_s(i):
        rows = at(i * BLK, BLK, BLK)
        return pltpu.make_async_copy(s_hbm.at[rows], sf.at[rows], ld.at[9 + i])

    for i in range(8):
        load_d(i).start()
    for i in range(8):
        load_s(i).start()

    partners = [to_core, to_xl, to_y(1), to_y(2), to_y(3), to_xh, to_z(1), to_z(2), to_z(3)]
    barrier = pltpu.get_barrier_semaphore()
    for device in partners:
        pl.semaphore_signal(barrier, inc=1, device_id=device, device_id_type=MESH)

    load_v.wait()

    def first_product(i):
        rows = at(((1 - c) * 4 + i) % 8 * BLK, BLK, BLK)
        return jnp.dot(d[rows, :], v[...], preferred_element_type=F32)

    def sib_block(i, carry):
        load_d(i).wait()
        part = first_product(i)
        rows = at(i * BLK, BLK, BLK)
        p_sib[0, rows, :] = part[:, :HALF]
        p_sib[1, rows, :] = part[:, HALF:]
        return carry

    lax.fori_loop(0, 4, sib_block, 0)
    pl.semaphore_wait(barrier, len(partners))
    core_copies = []
    for h in range(2):
        core_copies.append([
            send(p_sib.at[h, pl.ds(k * 512, 512)], r_core.at[h, pl.ds(k * 512, 512)], to_core)
            for k in range(2)
        ])

    def own_block(i, carry):
        load_d(4 + i).wait()
        part = first_product(4 + i)
        rows = at(i * BLK, BLK, BLK)
        q[0, rows, :] = part[:, :HALF]
        q[1, rows, :] = part[:, HALF:]
        return carry

    lax.fori_loop(0, 4, own_block, 0)

    a_own = lambda: at(z * 128, 128, 128)
    a_mine = lambda: at(z * 128 + xh * 64, 64, 64)
    a_theirs = lambda: at(z * 128 + (1 - xh) * 64, 64, 64)
    b_own = lambda: at(512 + xh * 256, 256, 256)
    b_mine = lambda: at(512 + xh * 256 + z * 64, 64, 64)

    def add_core(h, k):
        core_copies[h][k].wait_recv()
        rows = pl.ds(k * 512, 512)
        q[h, rows, :] += r_core[h, rows, :]

    def scatter_1(h):
        add_core(h, 0)
        az = [
            send(q.at[h, at((z + k) % 4 * 128, 128, 128)], r_az.at[h, k - 1], to_z(k))
            for k in (2, 1, 3)
        ]
        add_core(h, 1)
        bx = send(q.at[h, at(512 + (1 - xh) * 256, 256, 256)], r_bx.at[h], to_xh)
        return az, bx

    def scatter_2(h, az, bx):
        for copy in az:
            copy.wait_recv()
        q[h, a_own(), :] += r_az[h, 0] + r_az[h, 1] + r_az[h, 2]
        ax = send(q.at[h, a_theirs()], r_ax.at[h], to_xh)
        bx.wait_recv()
        q[h, b_own(), :] += r_bx[h]
        bz = [
            send(q.at[h, at(512 + xh * 256 + (z + k) % 4 * 64, 64, 64)], r_bz.at[h, k - 1], to_z(k))
            for k in (2, 1, 3)
        ]
        return ax, bz

    def global_rows(rows):
        return at(c * 1024 + rows.start, rows.size, 64)

    def piece(h, rows, device):
        ref = cf.at[h, global_rows(rows)]
        return send(ref, ref, device)

    def gather_1(h, ax, bz):
        ax.wait_recv()
        cf[h, global_rows(a_mine()), :] = q[h, a_mine(), :] + r_ax[h]
        g = {}
        g["ax"] = piece(h, a_mine(), to_xh)
        g["az"] = [piece(h, a_mine(), to_z(k)) for k in (2, 1, 3)]
        for copy in bz:
            copy.wait_recv()
        cf[h, global_rows(b_mine()), :] = q[h, b_mine(), :] + (r_bz[h, 0] + r_bz[h, 1] + r_bz[h, 2])
        g["bz"] = [piece(h, b_mine(), to_z(k)) for k in (2, 1, 3)]
        g["bx"] = [piece(h, b_mine(), to_xh)]
        g["core"] = [piece(h, a_mine(), to_core), piece(h, b_mine(), to_core)]
        return g

    def gather_2(h, g):
        g["ax"].wait_recv()
        g["az"] += [piece(h, a_theirs(), to_z(k)) for k in (2, 1, 3)]
        g["core"].append(piece(h, a_theirs(), to_core))
        for copy, k in zip(g["bz"], (2, 1, 3)):
            copy.wait_recv()
            rows = at(512 + xh * 256 + (z + 4 - k) % 4 * 64, 64, 64)
            g["bx"].append(piece(h, rows, to_xh))
            g["core"].append(piece(h, rows, to_core))

    def gather_3(h, g):
        for copy in g["az"]:
            copy.wait_recv()
        for k in (2, 1, 3):
            g["core"].append(piece(h, at((z + k) % 4 * 128, 128, 128), to_core))
        for copy in g["bx"]:
            copy.wait_recv()
        g["core"].append(piece(h, at(512 + (1 - xh) * 256, 256, 256), to_core))
        for copy in g["core"]:
            copy.wait_recv()
        for k in range(4):
            rows = pl.ds(k * 512, 512)
            whole = cf[h, rows, :]
            high = whole.astype(BF16)
            w[h, rows, :HALF] = high
            w[h, rows, HALF:] = (whole - high.astype(F32)).astype(BF16)

    def split(first, last):
        def body(i, carry):
            load_s(i).wait()
            for k in range(4):
                rows = at(i * BLK + k * 64, 64, 64)
                whole = sf[rows, :]
                high = whole.astype(BF16)
                s_hi[rows, :] = high
                s_lo[rows, :] = (whole - high.astype(F32)).astype(BF16)
            return carry

        lax.fori_loop(first, last, body, 0)

    sems_ya = [numbers(8) for _ in range(2)]
    sems_xb = [numbers(8) for _ in range(2)]

    def block_start(a, k):
        return (((xl + a) % 2) * 4 + (y + k) % 4) * BLK

    def copy_ya(h, a, k):
        return copy_of(
            m.at[h, at(block_start(a, k), 128, 128)], r_ya.at[h, a, k - 1],
            sems_ya[h] + a * 4 + k, to_y(k),
        )

    def copy_xb(h, k):
        return copy_of(
            m.at[h, at(block_start(1, k) + 128, 128, 128)], r_xb.at[h, k], sems_xb[h] + k, to_xl
        )

    def second_product(h, first, last):
        def body(i, carry):
            a, k = 1 - i // 4, (i + 1) % 4
            start = block_start(a, k)
            rows = at(start, BLK, BLK)
            part = jnp.dot(s_hi[rows, :], w[h], preferred_element_type=F32)
            low = jnp.dot(s_lo[rows, :], w[h, :, :HALF], preferred_element_type=F32)
            m[h, rows, :] = part[:, :HALF] + (part[:, HALF:] + low)

            @pl.when(k != 0)
            def _():
                copy_ya(h, a, k).start()

            @pl.when(a == 1)
            def _():
                copy_xb(h, k).start()

            return carry

        lax.fori_loop(first, last, body, 0)

    def reduce_1(h):
        yb = []
        for k in (1, 2, 3):
            copy_xb(h, k).wait_recv()
            r_xb[h, k] += m[h, at(block_start(0, k) + 128, 128, 128), :]
            yb.append(send(r_xb.at[h, k], r_yb.at[h, k - 1], to_y(k)))
        for k in (1, 2, 3):
            copy_ya(h, 1, k).wait_recv()
        m[h, at(block_start(1, 0), 128, 128), :] += r_ya[h, 1, 0] + r_ya[h, 1, 1] + r_ya[h, 1, 2]
        xa = send(m.at[h, at(block_start(1, 0), 128, 128)], r_xa.at[h], to_xl)
        return yb, xa

    def reduce_2(h, yb, xa):
        cols = pl.ds(h * HALF, HALF)
        for k in (1, 2, 3):
            copy_ya(h, 0, k).wait_recv()
        own = m[h, at(block_start(0, 0), 128, 128), :] + (r_ya[h, 0, 0] + r_ya[h, 0, 1] + r_ya[h, 0, 2])
        xa.wait_recv()
        o_ref[pl.ds(0, 128), cols] = own + r_xa[h]
        copy_xb(h, 0).wait_recv()
        own = m[h, at(block_start(0, 0) + 128, 128, 128), :] + r_xb[h, 0]
        for copy in yb:
            copy.wait_recv()
        o_ref[pl.ds(128, 128), cols] = own + (r_yb[h, 0] + r_yb[h, 1] + r_yb[h, 2])

    first_0 = scatter_1(0)
    first_1 = scatter_1(1)
    split(0, 3)
    second_0 = scatter_2(0, *first_0)
    split(3, 5)
    g0 = gather_1(0, *second_0)
    second_1 = scatter_2(1, *first_1)
    split(5, 6)
    gather_2(0, g0)
    split(6, 7)
    g1 = gather_1(1, *second_1)
    split(7, 8)
    gather_3(0, g0)
    second_product(0, 0, 3)
    gather_2(1, g1)
    second_product(0, 3, 8)
    gather_3(1, g1)
    second_product(1, 0, 4)
    tail_0 = reduce_1(0)
    second_product(1, 4, 8)
    tail_1 = reduce_1(1)
    reduce_2(0, *tail_0)
    reduce_2(1, *tail_1)

    for copy in sent:
        copy.wait_send()
    for h in range(2):
        for k in range(4):
            copy_xb(h, k).wait_send()
            if k:
                copy_ya(h, 0, k).wait_send()
                copy_ya(h, 1, k).wait_send()
    assert used[0] <= COPIES


def shards(dictionary, eigvecs, snapshots):
    vmem = pltpu.VMEM
    return pl.pallas_call(
        kernel,
        out_shape=jax.ShapeDtypeStruct((256, 256), F32),
        in_specs=[pl.BlockSpec(memory_space=pl.ANY)] * 3,
        out_specs=pl.BlockSpec(memory_space=pltpu.VMEM),
        scratch_shapes=[
            vmem((2048, 1024), BF16),
            vmem((1024, 256), BF16),
            vmem((2048, 2048), F32),
            vmem((2048, 2048), BF16),
            vmem((2048, 2048), BF16),
            vmem((2, 1024, HALF), F32),
            vmem((2, 1024, HALF), F32),
            vmem((2, 1024, HALF), F32),
            vmem((2, 3, 128, HALF), F32),
            vmem((2, 256, HALF), F32),
            vmem((2, 64, HALF), F32),
            vmem((2, 3, 64, HALF), F32),
            vmem((2, 2048, HALF), F32),
            vmem((2, 2048, 2 * HALF), BF16),
            vmem((2, 2048, HALF), F32),
            vmem((2, 2, 3, 128, HALF), F32),
            vmem((2, 4, 128, HALF), F32),
            vmem((2, 128, HALF), F32),
            vmem((2, 3, 128, HALF), F32),
            pltpu.SemaphoreType.DMA((17,)),
            pltpu.SemaphoreType.DMA((COPIES,)),
            pltpu.SemaphoreType.DMA((COPIES,)),
        ],
        compiler_params=pltpu.CompilerParams(
            collective_id=0, has_side_effects=True, vmem_limit_bytes=58 * 2**20
        ),
        cost_estimate=pl.CostEstimate(flops=10**10, bytes_accessed=22 * 2**20, transcendentals=0),
    )(dictionary, eigvecs, snapshots)


def solution(mesh):
    return jax.shard_map(
        shards,
        mesh=mesh,
        in_specs=(P("tm", "feat"), P("feat", None), P("feat", "tm")),
        out_specs=P(("feat", "tm"), None),
        check_vma=False,
    )
```

```python
import jax
import jax.numpy as jnp
from jax import lax
from jax.experimental import pallas as pl
from jax.experimental.pallas import tpu as pltpu
from jax.sharding import PartitionSpec as P

MESH = pl.DeviceIdType.MESH
F32, BF16 = jnp.float32, jnp.bfloat16
HALF = 128
BLK = 256
TALL = 512
EVENTS = 34
RING = (2, 1, 3)


def at(start, size, align):
    return pl.ds(pl.multiple_of(start, align), size)


def kernel(
    d_hbm, v_hbm, s_hbm, o_ref,
    d, v, sf, s_hi, s_lo, p_sib, q, r_core, r_az, r_bx, r_ax, r_bz, cf, w, m,
    r_ya, r_xb, r_xa, r_yb, ld, ss, rs,
):
    tm, ft = lax.axis_index("tm"), lax.axis_index("feat")
    xl, y = tm // 4, tm % 4
    z, xh, c = ft // 4, (ft // 2) % 2, ft % 2

    def to_z(k):
        return {"tm": tm, "feat": ((z + k) % 4) * 4 + xh * 2 + c}

    def to_y(k):
        return {"tm": xl * 4 + (y + k) % 4, "feat": ft}

    to_xh = {"tm": tm, "feat": z * 4 + (1 - xh) * 2 + c}
    to_xl = {"tm": (1 - xl) * 4 + y, "feat": ft}
    to_core = {"tm": tm, "feat": z * 4 + xh * 2 + (1 - c)}

    events = {}
    rows_sent = [0]

    def event(*name):
        return rs.at[events.setdefault(name, len(events))]

    def send(src, dst, device, *name, count=True):
        if count:
            rows_sent[0] += src.shape[0]
        pltpu.make_async_remote_copy(
            src_ref=src, dst_ref=dst, send_sem=ss.at[0], recv_sem=event(*name),
            device_id=device, device_id_type=MESH,
        ).start()

    def arrived(like, *name):
        pltpu.make_async_copy(like, like, event(*name)).wait()

    load_v = pltpu.make_async_copy(v_hbm, v, ld.at[0])

    def load_d(i):
        rows = at((2 * (1 - c) + i) % 4 * TALL, TALL, TALL)
        return pltpu.make_async_copy(d_hbm.at[rows], d.at[rows], ld.at[1 + i])

    def cells(i):
        a, k = 1 - i // 4, (i + 1) % 4
        return a, k, at((((xl + a) % 2) * 4 + (y + k) % 4) * BLK, BLK, BLK)

    def load_s(i):
        return pltpu.make_async_copy(
            s_hbm.at[cells(i)[2]], sf.at[pl.ds(i * BLK, BLK)], ld.at[5 + i // 2]
        )

    partners = [to_core, to_xl, to_y(1), to_y(2), to_y(3), to_xh, to_z(1), to_z(2), to_z(3)]
    barrier = pltpu.get_barrier_semaphore()
    for device in partners:
        pl.semaphore_signal(barrier, inc=1, device_id=device, device_id_type=MESH)
    load_v.start()
    for i in range(4):
        load_d(i).start()
    for i in range(8):
        load_s(i).start()

    def first_product(i, out, j):
        load_d(i).wait()
        rows = at((2 * (1 - c) + i) % 4 * TALL, TALL, TALL)
        part = jnp.dot(d[rows, :], v[...], preferred_element_type=F32)
        out[0, pl.ds(j * TALL, TALL), :] = part[:, :HALF]
        out[1, pl.ds(j * TALL, TALL), :] = part[:, HALF:]

    load_v.wait()
    first_product(0, p_sib, 0)
    pl.semaphore_wait(barrier, len(partners))

    def send_core(h, j):
        rows = pl.ds(j * TALL, TALL)
        send(p_sib.at[h, rows], r_core.at[h, rows], to_core, "core", h, j)

    send_core(0, 0)
    first_product(1, p_sib, 1)
    send_core(0, 1)
    send_core(1, 0)
    send_core(1, 1)
    first_product(2, q, 0)
    first_product(3, q, 1)

    def add_core(h, j):
        rows = pl.ds(j * TALL, TALL)
        arrived(r_core.at[h, rows], "core", h, j)
        q[h, rows, :] += r_core[h, rows, :]

    a_own = at(z * 128, 128, 128)
    a_mine = at(z * 128 + xh * 64, 64, 64)
    a_theirs = at(z * 128 + (1 - xh) * 64, 64, 64)
    b_own = at(512 + xh * 256, 256, 256)
    b_theirs = at(512 + (1 - xh) * 256, 256, 256)

    def b_at(k):
        return at(512 + xh * 256 + (z + k) % 4 * 64, 64, 64)

    def scatter_1(h):
        add_core(h, 0)
        for k in RING:
            send(q.at[h, at((z + k) % 4 * 128, 128, 128)], r_az.at[h, k - 1], to_z(k), "az", h)
        add_core(h, 1)
        send(q.at[h, b_theirs], r_bx.at[h], to_xh, "bx", h)

    def scatter_2(h):
        arrived(r_az.at[h], "az", h)
        q[h, a_own, :] += r_az[h, 0] + r_az[h, 1] + r_az[h, 2]
        send(q.at[h, a_theirs], r_ax.at[h], to_xh, "ax", h)
        arrived(r_bx.at[h], "bx", h)
        q[h, b_own, :] += r_bx[h]
        for k in RING:
            send(q.at[h, b_at(k)], r_bz.at[h, k - 1], to_z(k), "bz", h)

    def whole_rows(rows):
        return at(c * 1024 + rows.start, rows.size, 64)

    def share(h, rows, device, *name):
        ref = cf.at[h, whole_rows(rows)]
        send(ref, ref, device, *name)

    def gather_1(h):
        arrived(r_ax.at[h], "ax", h)
        cf[h, whole_rows(a_mine), :] = q[h, a_mine, :] + r_ax[h]
        share(h, a_mine, to_xh, "gax", h)
        for k in RING:
            share(h, a_mine, to_z(k), "gaz", h)
        arrived(r_bz.at[h], "bz", h)
        cf[h, whole_rows(b_at(0)), :] = q[h, b_at(0), :] + (r_bz[h, 0] + r_bz[h, 1] + r_bz[h, 2])
        for k in RING:
            share(h, b_at(0), to_z(k), "gbz", h)
        share(h, b_at(0), to_xh, "gbx", h)

    def gather_2(h):
        arrived(r_ax.at[h], "gax", h)
        for k in RING:
            share(h, a_theirs, to_z(k), "gaz", h)
        arrived(r_bz.at[h], "gbz", h)
        for k in RING:
            share(h, b_at(k), to_xh, "gbx", h)
        share(h, a_own, to_core, "gcore", h)
        share(h, b_own, to_core, "gcore", h)

    def gather_3(h):
        arrived(r_az.at[h], "gaz", h)
        for k in RING:
            share(h, at((z + k) % 4 * 128, 128, 128), to_core, "gcore", h)
        arrived(r_bx.at[h], "gbx", h)
        share(h, b_theirs, to_core, "gcore", h)

    def gather_4(h):
        arrived(r_core.at[h], "gcore", h)
        for k in range(4):
            rows = pl.ds(k * TALL, TALL)
            whole = cf[h, rows, :]
            high = whole.astype(BF16)
            w[h, rows, :HALF] = high
            w[h, rows, HALF:] = (whole - high.astype(F32)).astype(BF16)

    def split(j):
        load_s(2 * j).wait()
        load_s(2 * j + 1).wait()

        def body(i, carry):
            rows = at(j * TALL + i * 64, 64, 64)
            whole = sf[rows, :]
            high = whole.astype(BF16)
            s_hi[rows, :] = high
            s_lo[rows, :] = (whole - high.astype(F32)).astype(BF16)
            return carry

        lax.fori_loop(0, TALL // 64, body, 0)

    def second_product(h, first, last):
        for j in (0, 1, 2, 3):
            event("ya", h, j // 2)
            event("xb", h, j % 2)
        if first == 0:
            rows_sent[0] += 10 * 128

        def body(j, carry):
            rows = at(j * TALL, TALL, TALL)
            part = jnp.dot(s_hi[rows, :], w[h], preferred_element_type=F32)
            low = jnp.dot(s_lo[rows, :], w[h, :, :HALF], preferred_element_type=F32)
            m[h, rows, :] = part[:, :HALF] + (part[:, HALF:] + low)

            for a in (0, 1):

                @pl.when(j // 2 == 1 - a)
                def _():
                    for t in (0, 1):
                        k = (2 * j + t + 1) % 4

                        @pl.when(k != 0)
                        def _():
                            send(
                                m.at[h, at(j * TALL + t * BLK, 128, 128)], r_ya.at[h, a, k - 1],
                                to_y(k), "ya", h, a, count=False,
                            )

            for n in (0, 1):

                @pl.when(j == n)
                def _():
                    for t in (0, 1):
                        send(
                            m.at[h, pl.ds(n * TALL + t * BLK + 128, 128)], r_xb.at[h, 2 * n + t],
                            to_xl, "xb", h, n, count=False,
                        )

            return carry

        lax.fori_loop(first, last, body, 0)

    def reduce_1(h):
        for n in (0, 1):
            arrived(r_xb.at[h, pl.ds(2 * n, 2)], "xb", h, n)
            for i in ((0, 1), (2,))[n]:
                r_xb[h, i] += m[h, pl.ds((4 + i) * BLK + 128, 128), :]
                send(r_xb.at[h, i], r_yb.at[h, i], to_y(i + 1), "yb", h)
        arrived(r_ya.at[h, 1], "ya", h, 1)
        mine = pl.ds(3 * BLK, 128)
        m[h, mine, :] += r_ya[h, 1, 0] + r_ya[h, 1, 1] + r_ya[h, 1, 2]
        send(m.at[h, mine], r_xa.at[h], to_xl, "xa", h)

    def reduce_2(h):
        cols = pl.ds(h * HALF, HALF)
        arrived(r_ya.at[h, 0], "ya", h, 0)
        own = m[h, pl.ds(7 * BLK, 128), :] + (r_ya[h, 0, 0] + r_ya[h, 0, 1] + r_ya[h, 0, 2])
        arrived(r_xa.at[h], "xa", h)
        o_ref[pl.ds(0, 128), cols] = own + r_xa[h]
        own = m[h, pl.ds(7 * BLK + 128, 128), :] + r_xb[h, 3]
        arrived(r_yb.at[h], "yb", h)
        o_ref[pl.ds(128, 128), cols] = own + (r_yb[h, 0] + r_yb[h, 1] + r_yb[h, 2])

    scatter_1(0)
    scatter_1(1)
    split(0)
    scatter_2(0)
    split(1)
    scatter_2(1)
    gather_1(0)
    split(2)
    gather_1(1)
    gather_2(0)
    split(3)
    gather_2(1)
    gather_3(0)
    gather_4(0)
    second_product(0, 0, 2)
    gather_3(1)
    second_product(0, 2, 4)
    gather_4(1)
    second_product(1, 0, 2)
    reduce_1(0)
    second_product(1, 2, 4)
    reduce_1(1)
    reduce_2(0)
    reduce_2(1)

    everything = sf.at[pl.ds(0, rows_sent[0] // 16)]
    pltpu.make_async_copy(everything, everything, ss.at[0]).wait()
    assert len(events) == EVENTS and rows_sent[0] % 128 == 0


def shards(dictionary, eigvecs, snapshots):
    vmem = pltpu.VMEM
    return pl.pallas_call(
        kernel,
        out_shape=jax.ShapeDtypeStruct((256, 256), F32),
        in_specs=[pl.BlockSpec(memory_space=pl.ANY)] * 3,
        out_specs=pl.BlockSpec(memory_space=pltpu.VMEM),
        scratch_shapes=[
            vmem((2048, 1024), BF16),
            vmem((1024, 256), BF16),
            vmem((2048, 2048), F32),
            vmem((2048, 2048), BF16),
            vmem((2048, 2048), BF16),
            vmem((2, 1024, HALF), F32),
            vmem((2, 1024, HALF), F32),
            vmem((2, 1024, HALF), F32),
            vmem((2, 3, 128, HALF), F32),
            vmem((2, 256, HALF), F32),
            vmem((2, 64, HALF), F32),
            vmem((2, 3, 64, HALF), F32),
            vmem((2, 2048, HALF), F32),
            vmem((2, 2048, 2 * HALF), BF16),
            vmem((2, 2048, HALF), F32),
            vmem((2, 2, 3, 128, HALF), F32),
            vmem((2, 4, 128, HALF), F32),
            vmem((2, 128, HALF), F32),
            vmem((2, 3, 128, HALF), F32),
            pltpu.SemaphoreType.DMA((9,)),
            pltpu.SemaphoreType.DMA((1,)),
            pltpu.SemaphoreType.DMA((EVENTS,)),
        ],
        compiler_params=pltpu.CompilerParams(
            collective_id=0, has_side_effects=True, vmem_limit_bytes=58 * 2**20
        ),
        cost_estimate=pl.CostEstimate(flops=10**10, bytes_accessed=22 * 2**20, transcendentals=0),
    )(dictionary, eigvecs, snapshots)


def solution(mesh):
    return jax.shard_map(
        shards,
        mesh=mesh,
        in_specs=(P("tm", "feat"), P("feat", None), P("feat", "tm")),
        out_specs=P(("feat", "tm"), None),
        check_vma=False,
    )
```

```python
import jax
import jax.numpy as jnp
from jax import lax
from jax.experimental import pallas as pl
from jax.experimental.pallas import tpu as pltpu
from jax.sharding import PartitionSpec as P

MESH = pl.DeviceIdType.MESH
F32, BF16 = jnp.float32, jnp.bfloat16
HALF = 128
BLK = 256
TALL = 512
EVENTS = 38
RING = (2, 1, 3)
ORDER = (2, 1, 3, 0)
FIRST_X = (96, 96)


def at(start, size, align):
    return pl.ds(pl.multiple_of(start, align), size)


def kernel(
    d_hbm, v_hbm, s_hbm, o_ref,
    d, v, sf, s_hi, s_lo, p_sib, q, r_core, r_az, r_bx, r_ax, r_bz, cf, w, m,
    r_rl, r_ya, r_xb, r_xa, r_yb, ld, ss, rs,
):
    tm, ft = lax.axis_index("tm"), lax.axis_index("feat")
    xl, y = tm // 4, tm % 4
    z, xh, c = ft // 4, (ft // 2) % 2, ft % 2

    def to_zx(k, n):
        return {"tm": tm, "feat": ((z + k) % 4) * 4 + (xh + n) % 2 * 2 + c}

    def to_z(k):
        return to_zx(k, 0)

    def to_y(k):
        return {"tm": xl * 4 + (y + k) % 4, "feat": ft}

    to_xh = to_zx(0, 1)
    to_xl = {"tm": (1 - xl) * 4 + y, "feat": ft}
    to_core = {"tm": tm, "feat": z * 4 + xh * 2 + (1 - c)}

    events = {}
    rows_sent = [0]

    def event(*name):
        return rs.at[events.setdefault(name, len(events))]

    def send(src, dst, device, *name, count=True):
        if count:
            rows_sent[0] += src.shape[0]
        pltpu.make_async_remote_copy(
            src_ref=src, dst_ref=dst, send_sem=ss.at[0], recv_sem=event(*name),
            device_id=device, device_id_type=MESH,
        ).start()

    def arrived(like, *name):
        pltpu.make_async_copy(like, like, event(*name)).wait()

    load_v = pltpu.make_async_copy(v_hbm, v, ld.at[0])

    def half_rows(n):
        return at((xh + 1 + n) % 2 * TALL, TALL, TALL)

    def first_rows(i):
        owner = 1 - c if i < 2 else c
        return at((owner * 2 + (xh + 1 + i) % 2) * TALL, TALL, TALL)

    def load_d(i):
        rows = first_rows(i)
        return pltpu.make_async_copy(d_hbm.at[rows], d.at[rows], ld.at[1 + i])

    def cells(i):
        a, k = 1 - i // 4, ORDER[i % 4]
        return at((((xl + a) % 2) * 4 + (y + k) % 4) * BLK, BLK, BLK)

    def load_s(i):
        return pltpu.make_async_copy(
            s_hbm.at[cells(i)], sf.at[pl.ds(i * BLK, BLK)], ld.at[5 + i // 2]
        )

    partners = [to_core, to_xl, to_xh] + [to(k) for to in (to_y, to_z) for k in RING]
    barrier = pltpu.get_barrier_semaphore()
    for device in partners:
        pl.semaphore_signal(barrier, inc=1, device_id=device, device_id_type=MESH)
    load_v.start()
    for i in range(4):
        load_d(i).start()
    for i in range(8):
        load_s(i).start()

    def first_product(i, out):
        load_d(i).wait()
        part = jnp.dot(d[first_rows(i), :], v[...], preferred_element_type=F32)
        out[0, half_rows(i), :] = part[:, :HALF]
        out[1, half_rows(i), :] = part[:, HALF:]

    load_v.wait()
    first_product(0, p_sib)
    pl.semaphore_wait(barrier, len(partners))

    def send_core(h, j):
        rows = half_rows(j)
        send(p_sib.at[h, rows], r_core.at[h, rows], to_core, "core", h, j)

    send_core(0, 0)
    first_product(1, p_sib)
    send_core(0, 1)
    send_core(1, 0)
    send_core(1, 1)
    first_product(2, q)
    first_product(3, q)

    def add_core(h, j):
        rows = half_rows(j)
        arrived(r_core.at[h, rows], "core", h, j)
        q[h, rows, :] += r_core[h, rows, :]

    a_own = at(z * 128, 128, 128)
    a_mine = at(z * 128 + xh * 64, 64, 64)
    a_theirs = at(z * 128 + (1 - xh) * 64, 64, 64)
    b_own = at(512 + xh * 256, 256, 256)
    b_theirs = at(512 + (1 - xh) * 256, 256, 256)

    def b_at(k):
        return at(512 + xh * 256 + (z + k) % 4 * 64, 64, 64)

    def scatter_1(h):
        add_core(h, 0)
        add_core(h, 1)
        for k in RING:
            send(q.at[h, at((z + k) % 4 * 128, 128, 128)], r_az.at[h, k - 1], to_z(k), "az", h)
        send(q.at[h, b_theirs], r_bx.at[h], to_xh, "bx", h)

    def scatter_2(h):
        arrived(r_az.at[h], "az", h)
        q[h, a_own, :] += r_az[h, 0] + r_az[h, 1] + r_az[h, 2]
        send(q.at[h, a_theirs], r_ax.at[h], to_xh, "ax", h)
        arrived(r_bx.at[h], "bx", h)
        q[h, b_own, :] += r_bx[h]
        for k in RING:
            send(q.at[h, b_at(k)], r_bz.at[h, k - 1], to_z(k), "bz", h)

    def whole_rows(rows):
        return at(c * 1024 + rows.start, rows.size, 64)

    def share(h, rows, device, *name):
        ref = cf.at[h, whole_rows(rows)]
        send(ref, ref, device, *name)

    def gather_1(h):
        arrived(r_ax.at[h], "ax", h)
        cf[h, whole_rows(a_mine), :] = q[h, a_mine, :] + r_ax[h]
        share(h, a_mine, to_xh, "gax", h)
        for k in RING:
            share(h, a_mine, to_z(k), "gaz", h)
        arrived(r_bz.at[h], "bz", h)
        cf[h, whole_rows(b_at(0)), :] = q[h, b_at(0), :] + (r_bz[h, 0] + r_bz[h, 1] + r_bz[h, 2])
        for k in RING:
            share(h, b_at(0), to_z(k), "gbz", h)
        share(h, b_at(0), to_xh, "gbx", h)

    def gather_2(h):
        arrived(r_ax.at[h], "gax", h)
        for k in RING:
            share(h, a_theirs, to_z(k), "gaz", h)
        arrived(r_bz.at[h], "gbz", h)
        for k in RING:
            share(h, b_at(k), to_xh, "gbx", h)
        share(h, a_own, to_core, "gcore", h)
        share(h, b_own, to_core, "gcore", h)

    def gather_3(h):
        arrived(r_az.at[h], "gaz", h)
        for k in RING:
            share(h, at((z + k) % 4 * 128, 128, 128), to_core, "gcore", h)
        arrived(r_bx.at[h], "gbx", h)
        share(h, b_theirs, to_core, "gcore", h)

    def gather_4(h):
        arrived(r_core.at[h], "gcore", h)
        for k in range(4):
            rows = pl.ds(k * TALL, TALL)
            whole = cf[h, rows, :]
            high = whole.astype(BF16)
            w[h, rows, :HALF] = high
            w[h, rows, HALF:] = (whole - high.astype(F32)).astype(BF16)

    def split(j):
        load_s(2 * j).wait()
        load_s(2 * j + 1).wait()

        def body(i, carry):
            rows = at(j * TALL + i * 64, 64, 64)
            whole = sf[rows, :]
            high = whole.astype(BF16)
            s_hi[rows, :] = high
            s_lo[rows, :] = (whole - high.astype(F32)).astype(BF16)
            return carry

        lax.fori_loop(0, TALL // 64, body, 0)

    def lane(h):
        return (BLK - FIRST_X[h]) // 2

    def up(h, i):
        return pl.ds(i * BLK, lane(h))

    def down(h, i):
        return pl.ds(i * BLK + lane(h), lane(h))

    def by_y(h, i):
        return pl.ds(i * BLK, 2 * lane(h))

    def by_x(h, i):
        return pl.ds(i * BLK + 2 * lane(h), FIRST_X[h])

    def second_product(h, first, last):
        top, low_end, x_rows = pl.ds(0, lane(h)), pl.ds(lane(h), lane(h)), pl.ds(0, FIRST_X[h])
        for n in (0, 1):
            event("rl", h, n)
            event("ya", h, n)
            event("xb", h, n)

        def body(j, carry):
            rows = at(j * TALL, TALL, TALL)
            part = jnp.dot(s_hi[rows, :], w[h], preferred_element_type=F32)
            low = jnp.dot(s_lo[rows, :], w[h, :, :HALF], preferred_element_type=F32)
            m[h, rows, :] = part[:, :HALF] + (part[:, HALF:] + low)

            for n in range(first, last):

                @pl.when(j == n)
                def _():
                    a, i = 1 - n // 2, 2 * n
                    if n % 2 == 0:
                        for t, src, k in ((0, up(h, i), 1), (1, down(h, i), 3)):
                            send(m.at[h, src], r_rl.at[h, a, t, top], to_y(k), "rl", h, a, count=False)
                        src, dst, k = down(h, i + 1), r_ya.at[h, a, 0, low_end], 1
                    else:
                        src, dst, k = up(h, i), r_ya.at[h, a, 1, top], 3
                    send(m.at[h, src], dst, to_y(k), "ya", h, a, count=False)
                    if a == 1:
                        for t in (i, i + 1):
                            send(
                                m.at[h, by_x(h, t)], r_xb.at[h, t, x_rows], to_xl,
                                "xb", h, n, count=False,
                            )

            return carry

        lax.fori_loop(first, last, body, 0)
        for n in range(first, last):
            rows_sent[0] += (3 if n % 2 == 0 else 1) * lane(h) + (2 * FIRST_X[h] if n < 2 else 0)

    def relay(h, a):
        top, low_end = pl.ds(0, lane(h)), pl.ds(lane(h), lane(h))
        arrived(r_rl.at[h, a, :, top], "rl", h, a)
        i = 4 * (1 - a)
        m[h, up(h, i + 1), :] += r_rl[h, a, 0, top, :]
        send(m.at[h, up(h, i + 1)], r_ya.at[h, a, 0, top], to_y(1), "ya", h, a)
        m[h, down(h, i + 2), :] += r_rl[h, a, 1, top, :]
        send(m.at[h, down(h, i + 2)], r_ya.at[h, a, 1, low_end], to_y(3), "ya", h, a)

    def reduce_x(h, n):
        x_rows = pl.ds(0, FIRST_X[h])
        arrived(r_xb.at[h, pl.ds(2 * n, 2), x_rows], "xb", h, n)
        for i in ((0, 1), (2,))[n]:
            r_xb[h, i, x_rows, :] += m[h, by_x(h, 4 + i), :]
            send(r_xb.at[h, i, x_rows], r_yb.at[h, i, x_rows], to_y(ORDER[i]), "yb", h)

    def reduce_y(h):
        rows, mine = pl.ds(0, 2 * lane(h)), by_y(h, 3)
        arrived(r_ya.at[h, 1, :, rows], "ya", h, 1)
        m[h, mine, :] += r_ya[h, 1, 0, rows, :] + r_ya[h, 1, 1, rows, :]
        send(m.at[h, mine], r_xa.at[h, rows], to_xl, "xa", h)

    def reduce_end(h):
        cols = pl.ds(h * HALF, HALF)
        rows, x_rows = pl.ds(0, 2 * lane(h)), pl.ds(0, FIRST_X[h])
        arrived(r_yb.at[h, :, x_rows], "yb", h)
        own = m[h, by_x(h, 7), :] + r_xb[h, 3, x_rows, :]
        o_ref[pl.ds(2 * lane(h), FIRST_X[h]), cols] = own + (
            r_yb[h, 0, x_rows, :] + r_yb[h, 1, x_rows, :] + r_yb[h, 2, x_rows, :]
        )
        arrived(r_ya.at[h, 0, :, rows], "ya", h, 0)
        own = m[h, by_y(h, 7), :] + (r_ya[h, 0, 0, rows, :] + r_ya[h, 0, 1, rows, :])
        arrived(r_xa.at[h, rows], "xa", h)
        o_ref[rows, cols] = own + r_xa[h, rows, :]

    scatter_1(0)
    scatter_1(1)
    split(0)
    split(1)
    split(2)
    split(3)
    scatter_2(0)
    scatter_2(1)
    gather_1(0)
    gather_1(1)
    gather_2(0)
    gather_2(1)
    gather_3(0)
    gather_4(0)
    second_product(0, 0, 1)
    gather_3(1)
    second_product(0, 1, 4)
    relay(0, 1)
    gather_4(1)
    second_product(1, 0, 1)
    relay(0, 0)
    reduce_x(0, 0)
    second_product(1, 1, 2)
    reduce_y(0)
    reduce_x(0, 1)
    second_product(1, 2, 3)
    relay(1, 1)
    second_product(1, 3, 4)
    reduce_x(1, 0)
    relay(1, 0)
    reduce_x(1, 1)
    reduce_y(1)
    reduce_end(0)
    reduce_end(1)

    everything = sf.at[pl.ds(0, rows_sent[0] // 16)]
    pltpu.make_async_copy(everything, everything, ss.at[0]).wait()
    assert len(events) == EVENTS and rows_sent[0] % 128 == 0, (len(events), rows_sent)


def shards(dictionary, eigvecs, snapshots):
    vmem = pltpu.VMEM
    return pl.pallas_call(
        kernel,
        out_shape=jax.ShapeDtypeStruct((256, 256), F32),
        in_specs=[pl.BlockSpec(memory_space=pl.ANY)] * 3,
        out_specs=pl.BlockSpec(memory_space=pltpu.VMEM),
        scratch_shapes=[
            vmem((2048, 1024), BF16),
            vmem((1024, 256), BF16),
            vmem((2048, 2048), F32),
            vmem((2048, 2048), BF16),
            vmem((2048, 2048), BF16),
            vmem((2, 1024, HALF), F32),
            vmem((2, 1024, HALF), F32),
            vmem((2, 1024, HALF), F32),
            vmem((2, 3, 128, HALF), F32),
            vmem((2, 256, HALF), F32),
            vmem((2, 64, HALF), F32),
            vmem((2, 3, 64, HALF), F32),
            vmem((2, 2048, HALF), F32),
            vmem((2, 2048, 2 * HALF), BF16),
            vmem((2, 2048, HALF), F32),
            vmem((2, 2, 2, 96, HALF), F32),
            vmem((2, 2, 2, 192, HALF), F32),
            vmem((2, 4, 128, HALF), F32),
            vmem((2, 192, HALF), F32),
            vmem((2, 3, 128, HALF), F32),
            pltpu.SemaphoreType.DMA((9,)),
            pltpu.SemaphoreType.DMA((1,)),
            pltpu.SemaphoreType.DMA((EVENTS,)),
        ],
        compiler_params=pltpu.CompilerParams(
            collective_id=0, has_side_effects=True, vmem_limit_bytes=54720 * 2**10
        ),
        cost_estimate=pl.CostEstimate(flops=10**10, bytes_accessed=22 * 2**20, transcendentals=0),
    )(dictionary, eigvecs, snapshots)


def solution(mesh):
    return jax.shard_map(
        shards,
        mesh=mesh,
        in_specs=(P("tm", "feat"), P("feat", None), P("feat", "tm")),
        out_specs=P(("feat", "tm"), None),
        check_vma=False,
    )
```
